32 devices in a mesh: outer: 4 (over y, x), inner: 8 (over z, core).
Axes of the slice: x: 2, y: 2, z: 4, core: 2. Of those that a mesh axis runs over, the one named last changes fastest.
Arguments:
- queries: bfloat16 [49152, 2048], P(('outer', 'inner')), may hold values from -6 to 6
- keys: bfloat16 [49152, 2048], P(('outer', 'inner')), may hold values from -6 to 6
- values: bfloat16 [49152, 2048], P(('outer', 'inner')), may hold values from -6 to 6
- gain: float32 [2048], replicated, may hold values from 0.5 to 1.5
- tile_doc: int32 [384], P(('outer', 'inner')), may hold values from 0 to 7, as said below
- tile_fill: int32 [384], P(('outer', 'inner')), may hold values from 1 to 128, as said below
Outputs:
- attended: bfloat16 [49152, 2048], P(('outer', 'inner'))
The draws below stay inside these ranges and needn't reach their ends.
Inputs may be any that keep to these rules, and one draw needn't show every extreme that they name: tile_doc is 0 at the first tile and rises by 0 or 1 from each tile to the next, so each document holds whole consecutive tiles; the window holds exactly 8 documents. tile_fill is 128 on every tile except the last tile of each document.
All inputs are finite; a program needn't handle non-finite values.
Results may differ from the reference program's by a relative error of at most 0.0027.
Values sent between devices are 32-bit elements; how exact they have to be, the bound alone decides.
A program may use at most 192 MiB of HBM per device.

```python
import jax
import jax.numpy as jnp
from jax import lax

HEADS = 16
HEAD = 128
TILE = 128
BLOCK = 512
TOK_DEV = 1536
TOKENS = 49152
TILES = 384


def doc_layout(key):
    documents = TILES * 32 // TOK_DEV
    span = TILES * 5 // 8
    rest = TILES - span
    order = jax.random.permutation(jax.random.fold_in(key, 11), rest - 1) + 1
    starts = order[:documents - 1]
    marks = jnp.zeros((rest,), jnp.int32).at[starts].set(1)
    marks = marks.at[0].set(1)
    rest_docs = jnp.cumsum(marks) - 1
    split = jax.random.randint(jax.random.fold_in(key, 13), (), 1, rest + 1)
    places = jnp.arange(TILES, dtype=jnp.int32)
    source = jnp.where(places < split, places, jnp.where(places < split + span, split - 1, places - span))
    docs = rest_docs[source].astype(jnp.int32)
    ending = jnp.concatenate([docs[1:] != docs[:-1], jnp.ones((1,), bool)])
    partial_fill = jax.random.randint(jax.random.fold_in(key, 12), (TILES,), 1, TILE + 1)
    fill = jnp.where(ending, partial_fill, TILE).astype(jnp.int32)
    return (docs, fill)


def draw_tile_doc(key, part):
    return doc_layout(key)[0]


def draw_tile_fill(key, part):
    return doc_layout(key)[1]


def shard_levels(key, dims, shards, low, top_value):
    loudness = 1.0
    for position, blocks in shards:
        draws = jax.random.uniform(jax.random.fold_in(jax.random.fold_in(key, 6), position), (blocks,), jnp.float32, low / len(shards), top_value / len(shards))
        loudness = loudness * jnp.repeat(jnp.exp(draws), dims[position] // blocks).reshape((-1,) + (1,) * (len(dims) - 1 - position))
    return loudness


def centred(own_key, shape, spread, reach, cuts=(), kind=jnp.bfloat16):
    values = spread * jax.random.normal(own_key, shape, jnp.float32)
    if cuts:
        values = values * shard_levels(own_key, shape, cuts, -0.22, 0.18)
    return jnp.clip(values, -reach, reach).astype(kind)


def setup_inputs(seed: int = 0) -> dict:
    seeds = jax.random.split(jax.random.key(seed), 7)
    return {
        "queries": centred(seeds[0], (TOKENS, HEADS * HEAD), 1.0, 6.0, ((0, 32),)),
        "keys": centred(seeds[1], (TOKENS, HEADS * HEAD), 1.0, 6.0, ((0, 32),)),
        "values": centred(seeds[2], (TOKENS, HEADS * HEAD), 1.0, 6.0, ((0, 32),)),
        "gain": jnp.clip(1.0 + 0.1 * jax.random.normal(seeds[3], (HEADS * HEAD,), jnp.float32), 0.5, 1.5),
        "tile_doc": draw_tile_doc(jax.random.fold_in(seeds[6], 71), 0),
        "tile_fill": draw_tile_fill(jax.random.fold_in(seeds[6], 71), 0),
    }


def combine(first, second):
    first_state, first_last, first_single = first
    second_state, second_last, second_single = second
    second_none = second_last[0] == 0
    first_none = first_last[0] == 0
    keep = jnp.logical_or(second_none, jnp.logical_and(second_single[0] == 1, second_last[0] == first_last[0]))
    state = jnp.where(keep, second_state + first_state, second_state)
    last = jnp.where(second_none, first_last, second_last)
    same = (first_last == second_last).astype(jnp.int32)
    single = jnp.where(second_none, first_single, jnp.where(first_none, second_single, first_single * second_single * same))
    return (state, last, single)

def summarize(key_rows, value_rows, docs, real):
    last_doc = docs[-1]
    chosen = jnp.logical_and(docs == last_doc, real)
    masked = jnp.where(chosen[:, None, None], key_rows, jnp.zeros_like(key_rows))
    state = jnp.einsum('thd,the->hde', masked.astype(jnp.float32), value_rows.astype(jnp.float32), precision=lax.Precision.HIGHEST)
    last = (last_doc + 1).reshape(1).astype(jnp.int32)
    single = (docs[0] == last_doc).astype(jnp.int32).reshape(1)
    return (state, last, single)

def block_output(query_rows, key_rows, value_rows, docs, real, carry, gain):
    length = query_rows.shape[0]
    scores = jnp.einsum('qhd,khd->hqk', query_rows.astype(jnp.float32), key_rows.astype(jnp.float32), precision=lax.Precision.HIGHEST)
    places = jnp.arange(length)
    allowed = (places[:, None] >= places[None, :]) & (docs[:, None] == docs[None, :]) & real[None, :]
    weights = jnp.where(allowed[None], scores, 0.0).astype(jnp.bfloat16)
    direct = jnp.einsum('hqk,khd->qhd', weights.astype(jnp.float32), value_rows.astype(jnp.float32), precision=lax.Precision.HIGHEST)
    state, last, single = carry
    carried = jnp.einsum('qhd,hde->qhe', query_rows.astype(jnp.float32), state, precision=lax.Precision.HIGHEST)
    uses = docs + 1 == last[0]
    raw = direct + jnp.where(uses[:, None, None], carried, 0.0)
    raw = jnp.where(real[:, None, None], raw, 0.0)
    meansq = lax.optimization_barrier(jnp.mean(raw * raw, axis=-1, keepdims=True))
    normed = raw * lax.rsqrt(meansq + 1e-06) * gain.reshape(HEADS, HEAD)
    return normed.astype(jnp.bfloat16)

def reference(queries, keys, values, gain, tile_doc, tile_fill):
    count = TOKENS // BLOCK
    docs = jnp.repeat(tile_doc, TILE).astype(jnp.int32)
    offsets = jnp.tile(jnp.arange(TILE, dtype=jnp.int32), TILES)
    real = offsets < jnp.repeat(tile_fill, TILE)
    query_blocks = queries.reshape(count, BLOCK, HEADS, HEAD)
    key_blocks = keys.reshape(count, BLOCK, HEADS, HEAD)
    value_blocks = values.reshape(count, BLOCK, HEADS, HEAD)
    doc_blocks = docs.reshape(count, BLOCK)
    real_blocks = real.reshape(count, BLOCK)
    start = (jnp.zeros((HEADS, HEAD, HEAD), jnp.float32), jnp.zeros((1,), jnp.int32), jnp.zeros((1,), jnp.int32))

    def advance(carry, items):
        query_rows, key_rows, value_rows, block_docs, block_real = items
        result = block_output(query_rows, key_rows, value_rows, block_docs, block_real, carry, gain)
        summary = summarize(key_rows, value_rows, block_docs, block_real)
        return (combine(carry, summary), result)
    final, outputs = lax.scan(advance, start, (query_blocks, key_blocks, value_blocks, doc_blocks, real_blocks))
    return outputs.reshape(TOKENS, HEADS * HEAD)
```

```python
import functools

import jax
import jax.numpy as jnp
from jax import lax
from jax.experimental import pallas as pl
from jax.experimental.pallas import tpu as pltpu
from jax.sharding import PartitionSpec as P

HEAD = 128
TILE = 128
BLOCK = 512
HALF_BLOCK = 256
PER = BLOCK // TILE
MESH = pl.DeviceIdType.MESH
F32 = jnp.float32
BF16 = jnp.bfloat16


def dot(a, b, dims):
    return lax.dot_general(a, b, (dims, ((), ())), preferred_element_type=F32)


def rows_below(limit):
    rows = lax.broadcasted_iota(jnp.int32, (TILE, HEAD), 0)
    return (rows < limit).astype(F32).astype(BF16)


def state_kernel(tiles, per_step, doc_ref, fill_ref, key_ref, value_ref, state_ref, mask_ref):
    @pl.when(pl.program_id(0) == 0)
    def _():
        for tile in range(tiles):
            limit = jnp.where(doc_ref[tile] == doc_ref[tiles - 1], fill_ref[tile], 0)
            mask_ref[pl.ds(tile * TILE, TILE), :] = rows_below(limit)

    for head in range(per_step):
        cols = slice(head * HEAD, (head + 1) * HEAD)
        masked = value_ref[:, cols] * mask_ref[...]
        state_ref[cols, :] = dot(key_ref[:, cols], masked, ((0,), (0,)))


def own_state(keys, values, tile_doc, tile_fill):
    length, width = keys.shape
    heads = width // HEAD
    per_step = 2
    block = pl.BlockSpec((length, per_step * HEAD), lambda h: (0, h))
    smem = pl.BlockSpec(memory_space=pltpu.SMEM)
    return pl.pallas_call(
        functools.partial(state_kernel, length // TILE, per_step),
        grid=(heads // per_step,),
        in_specs=[smem, smem, block, block],
        out_specs=pl.BlockSpec((per_step * HEAD, HEAD), lambda h: (h, 0)),
        out_shape=jax.ShapeDtypeStruct((width, HEAD), F32),
        scratch_shapes=[pltpu.VMEM((length, HEAD), BF16)],
        compiler_params=pltpu.CompilerParams(vmem_limit_bytes=32 * 1024 * 1024),
        name="own_state",
    )(tile_doc, tile_fill, keys, values)


def carry_kernel(
    outer, inner, tiles, half,
    doc_ref, state_ref, carry_ref, prev_ref,
    swap_out, swap_in, out1, in1, out3, in3, joined, back_out, back_in,
    swap_sems, send1, recv1, send3, recv3, back_sems,
):
    chips = outer * inner // 2
    part = half // chips
    me = lax.axis_index("outer") * inner + lax.axis_index("inner")
    chip = me // 2
    core = me % 2

    def place(device):
        return (device // inner, device % inner)

    def ahead(k):
        return (chip + k) % chips

    twin = place(chip * 2 + 1 - core)
    barrier = pltpu.get_barrier_semaphore()
    pl.semaphore_signal(barrier, inc=1, device_id=twin, device_id_type=MESH)

    def greet(k, _):
        pl.semaphore_signal(
            barrier, inc=1, device_id=place(ahead(k) * 2 + core), device_id_type=MESH
        )
        return 0

    lax.fori_loop(1, chips, greet, 0)

    my_doc = jnp.full((8, HEAD), doc_ref[tiles - 1], jnp.int32).astype(F32)
    swap_out[pl.ds(0, half), :] = state_ref[pl.ds((1 - core) * half, half), :]
    swap_out[pl.ds(half, 8), :] = my_doc
    pl.semaphore_wait(barrier, chips)

    swap = pltpu.make_async_remote_copy(
        swap_out, swap_in, swap_sems.at[0], swap_sems.at[1], device_id=twin, device_id_type=MESH
    )
    swap.start()
    swap.wait()

    first_core = core == 0
    their_doc = swap_in[pl.ds(half, 8), :]
    doc0 = jnp.where(first_core, my_doc, their_doc)
    doc1 = jnp.where(first_core, their_doc, my_doc)
    keep1 = (doc0 == doc1).astype(F32)[0:1, :]

    def pack(j, _):
        mine = state_ref[pl.ds(core * half + j * part, part), :]
        theirs = swap_in[pl.ds(j * part, part), :]
        state0 = jnp.where(first_core, mine, theirs)
        state1 = jnp.where(first_core, theirs, mine)
        slot = (j - chip + chips) % chips
        out1[slot, pl.ds(0, part), :] = state1 + keep1 * state0
        out1[slot, pl.ds(part, 8), :] = doc1
        return 0

    lax.fori_loop(0, chips, pack, 0)

    def copy1(k):
        return pltpu.make_async_remote_copy(
            out1.at[k], in1.at[k], send1.at[k], recv1.at[k],
            device_id=place(ahead(k) * 2 + core), device_id_type=MESH,
        )

    def copy3(k):
        return pltpu.make_async_remote_copy(
            out3.at[k], in3.at[k], send3.at[k], recv3.at[k],
            device_id=place(ahead(k) * 2 + core), device_id_type=MESH,
        )

    def run(action):
        def step(k, _):
            action(k)
            return 0

        lax.fori_loop(1, chips, step, 0)

    run(lambda k: copy1(k).start())
    in1[0] = out1[0]
    run(lambda k: copy1(k).wait())

    def lap(c, so_far):
        total, doc = so_far
        to = (c - chip + chips) % chips
        slot = (chip - c + chips) % chips
        out3[to, pl.ds(0, part), :] = total
        out3[to, pl.ds(part, 8), :] = doc
        new_doc = in1[slot, pl.ds(part, 8), :]
        keep = (new_doc == doc).astype(F32)[0:1, :]
        return (in1[slot, pl.ds(0, part), :] + keep * total, new_doc)

    lax.fori_loop(
        0, chips, lap, (jnp.zeros((part, HEAD), F32), jnp.full((8, HEAD), -1.0, F32))
    )

    run(lambda k: copy3(k).start())
    in3[0] = out3[0]
    run(lambda k: copy3(k).wait())

    before = in3[0, pl.ds(part, 8), :]
    keep0 = (doc0 == before).astype(F32)[0:1, :]
    prev_ref[...] = jnp.where(first_core, before, doc0)

    def unpack(k, _):
        source = (chip - k + chips) % chips
        entering = in3[k, pl.ds(0, part), :]
        rows = pl.ds(source * part, part)
        mine = state_ref[pl.ds(core * half + source * part, part), :]
        state0 = jnp.where(first_core, mine, swap_in[rows, :])
        between = state0 + keep0 * entering
        joined[rows, :] = jnp.where(first_core, entering, between)
        back_out[rows, :] = jnp.where(first_core, between, entering)
        return 0

    lax.fori_loop(0, chips, unpack, 0)
    back = pltpu.make_async_remote_copy(
        back_out, back_in, back_sems.at[0], back_sems.at[1], device_id=twin, device_id_type=MESH
    )
    back.start()
    carry_ref[pl.ds(core * half, half), :] = joined[...]
    back.wait()
    carry_ref[pl.ds((1 - core) * half, half), :] = back_in[...]


def entering_state(mesh, state, tile_doc):
    outer, inner = mesh.shape["outer"], mesh.shape["inner"]
    chips = outer * inner // 2
    half = state.shape[0] // 2
    part = half // chips
    vmem = pl.BlockSpec(memory_space=pltpu.VMEM)
    slots = pltpu.VMEM((chips, part + 8, HEAD), F32)
    sems = pltpu.SemaphoreType.DMA((chips,))
    pair = pltpu.SemaphoreType.DMA((2,))
    return pl.pallas_call(
        functools.partial(carry_kernel, outer, inner, tile_doc.shape[0], half),
        in_specs=[pl.BlockSpec(memory_space=pltpu.SMEM), vmem],
        out_specs=[vmem, vmem],
        out_shape=[
            jax.ShapeDtypeStruct(state.shape, F32),
            jax.ShapeDtypeStruct((8, HEAD), F32),
        ],
        scratch_shapes=[
            pltpu.VMEM((half + 8, HEAD), F32),
            pltpu.VMEM((half + 8, HEAD), F32),
            slots, slots, slots, slots,
            pltpu.VMEM((half, HEAD), F32),
            pltpu.VMEM((half, HEAD), F32),
            pltpu.VMEM((half, HEAD), F32),
            pair, sems, sems, sems, sems, pair,
        ],
        compiler_params=pltpu.CompilerParams(
            collective_id=0, has_side_effects=True, vmem_limit_bytes=32 * 1024 * 1024
        ),
        name="entering_state",
    )(tile_doc, state)


def split(value):
    high = value.astype(BF16)
    return high, (value - high.astype(F32)).astype(BF16)


def attend_kernel(
    tiles, per_step,
    doc_ref, fill_ref, prev_ref, query_ref, key_ref, value_ref, carry_ref, gain_ref, out_ref,
    real_ref, last_ref, uses_ref, pair_ref,
):
    blocks = tiles // PER

    @pl.when(pl.program_id(0) == 0)
    def _():
        entering = prev_ref[0:1, :]
        for tile in range(tiles):
            block = tile // PER
            rows = pl.ds(tile * TILE, TILE)
            doc = doc_ref[tile]
            real = rows_below(fill_ref[tile])
            real_ref[rows, :] = real
            last_ref[rows, :] = rows_below(
                jnp.where(doc == doc_ref[block * PER + PER - 1], fill_ref[tile], 0)
            )
            if block == 0:
                same = (jnp.full((1, HEAD), doc, jnp.int32).astype(F32) == entering).astype(F32)
                uses_ref[rows, :] = (real.astype(F32) * same).astype(BF16)
            else:
                uses_ref[rows, :] = rows_below(
                    jnp.where(doc == doc_ref[block * PER - 1], fill_ref[tile], 0)
                )
        above = lax.broadcasted_iota(jnp.int32, (TILE, TILE), 0)
        across = lax.broadcasted_iota(jnp.int32, (TILE, TILE), 1)
        lower = (above >= across).astype(F32).astype(BF16)
        for block in range(blocks):
            for i in range(PER):
                for j in range(PER):
                    spot = (block, slice(i * TILE, (i + 1) * TILE), slice(j * TILE, (j + 1) * TILE))
                    if j > i:
                        pair_ref[spot] = jnp.zeros((TILE, TILE), BF16)
                    elif j == i:
                        pair_ref[spot] = lower
                    else:
                        same = doc_ref[block * PER + i] == doc_ref[block * PER + j]
                        pair_ref[spot] = rows_below(jnp.where(same, TILE, 0))

    for head in range(per_step):
        cols = slice(head * HEAD, (head + 1) * HEAD)
        gain = gain_ref[:, cols]
        carry = carry_ref[cols, :]
        for block in range(blocks):
            rows = slice(block * BLOCK, (block + 1) * BLOCK)
            query = query_ref[rows, cols] * real_ref[rows, :]
            key = key_ref[rows, cols]
            plain = value_ref[rows, cols]
            value = plain * real_ref[rows, :]
            high, low = split(carry)
            for part in range(BLOCK // HALF_BLOCK):
                begin = part * HALF_BLOCK
                end = begin + HALF_BLOCK
                scores = dot(query[begin:end], key[:end], ((1,), (1,)))
                weights = scores.astype(BF16) * pair_ref[block, begin:end, :end]
                raw = dot(weights, value[:end], ((1,), (0,)))
                place = slice(block * BLOCK + begin, block * BLOCK + end)
                using = query[begin:end] * uses_ref[place, :]
                raw = raw + (dot(using, high, ((1,), (0,))) + dot(using, low, ((1,), (0,))))
                meansq = jnp.mean(raw * raw, axis=-1, keepdims=True)
                normed = raw * lax.rsqrt(meansq + 1e-06) * gain
                out_ref[place, cols] = normed.astype(BF16)
            if block < blocks - 1:
                own = dot(key, plain * last_ref[rows, :], ((0,), (0,)))
                closing = doc_ref[block * PER + PER - 1]
                if block == 0:
                    closing = jnp.full((1, HEAD), closing, jnp.int32).astype(F32)
                    keep = (closing == prev_ref[0:1, :]).astype(F32)
                else:
                    keep = (closing == doc_ref[block * PER - 1]).astype(F32)
                carry = own + keep * carry


def attend(queries, keys, values, gain, tile_doc, tile_fill, carry, prev):
    length, width = queries.shape
    heads = width // HEAD
    per_step = 2
    block = pl.BlockSpec((length, per_step * HEAD), lambda h: (0, h))
    smem = pl.BlockSpec(memory_space=pltpu.SMEM)
    mask = pltpu.VMEM((length, HEAD), BF16)
    return pl.pallas_call(
        functools.partial(attend_kernel, length // TILE, per_step),
        grid=(heads // per_step,),
        in_specs=[
            smem,
            smem,
            pl.BlockSpec((8, HEAD), lambda h: (0, 0)),
            block,
            block,
            block,
            pl.BlockSpec((per_step * HEAD, HEAD), lambda h: (h, 0)),
            pl.BlockSpec((1, per_step * HEAD), lambda h: (0, h)),
        ],
        out_specs=block,
        out_shape=jax.ShapeDtypeStruct((length, width), BF16),
        scratch_shapes=[mask, mask, mask, pltpu.VMEM((length // BLOCK, BLOCK, BLOCK), BF16)],
        compiler_params=pltpu.CompilerParams(vmem_limit_bytes=48 * 1024 * 1024),
        name="attend",
    )(tile_doc, tile_fill, prev, queries, keys, values, carry, gain.reshape(1, width))


def solution(mesh):
    def body(queries, keys, values, gain, tile_doc, tile_fill):
        state = own_state(keys, values, tile_doc, tile_fill)
        carry, prev = entering_state(mesh, state, tile_doc)
        return attend(queries, keys, values, gain, tile_doc, tile_fill, carry, prev)

    rows = P(("outer", "inner"), None)
    tiles = P(("outer", "inner"))
    return jax.shard_map(
        body, mesh=mesh, in_specs=(rows, rows, rows, P(), tiles, tiles), out_specs=rows,
        check_vma=False,
    )
```

```python
import functools

import jax
import jax.numpy as jnp
from jax import lax
from jax.experimental import pallas as pl
from jax.experimental.pallas import tpu as pltpu
from jax.sharding import PartitionSpec as P

HEAD = 128
TILE = 128
BLOCK = 512
HALF_BLOCK = 256
PER = BLOCK // TILE
MESH = pl.DeviceIdType.MESH
F32 = jnp.float32
BF16 = jnp.bfloat16


def dot(a, b, dims):
    return lax.dot_general(a, b, (dims, ((), ())), preferred_element_type=F32)


def rows_below(limit):
    rows = lax.broadcasted_iota(jnp.int32, (TILE, HEAD), 0)
    return (rows < limit).astype(F32).astype(BF16)


def split(value):
    high = value.astype(BF16)
    return high, (value - high.astype(F32)).astype(BF16)


def build_masks(tiles, doc_ref, fill_ref, real_ref, last_ref, uses_ref, pair_ref):
    for tile in range(tiles):
        block = tile // PER
        rows = pl.ds(tile * TILE, TILE)
        doc = doc_ref[tile]
        fill = fill_ref[tile]
        real_ref[rows, :] = rows_below(fill)
        closing = doc_ref[block * PER + PER - 1]
        last_ref[rows, :] = rows_below(jnp.where(doc == closing, fill, 0))
        if block > 0:
            opening = doc_ref[block * PER - 1]
            uses_ref[rows, :] = rows_below(jnp.where(doc == opening, fill, 0))
    above = lax.broadcasted_iota(jnp.int32, (TILE, TILE), 0)
    across = lax.broadcasted_iota(jnp.int32, (TILE, TILE), 1)
    lower = (above >= across).astype(F32).astype(BF16)
    for block in range(tiles // PER):
        for i in range(PER):
            for j in range(PER):
                spot = (block, pl.ds(i * TILE, TILE), pl.ds(j * TILE, TILE))
                if j > i:
                    pair_ref[spot] = jnp.zeros((TILE, TILE), BF16)
                elif j == i:
                    pair_ref[spot] = lower
                else:
                    same = doc_ref[block * PER + i] == doc_ref[block * PER + j]
                    pair_ref[spot] = rows_below(jnp.where(same, TILE, 0))


def local_kernel(
    outer, inner, tiles, heads, chunks,
    doc_ref, fill_ref, query_hbm, key_hbm, value_hbm, raw_hbm, carry_ref, prev_ref,
    query_ref, key_ref, value_ref, raw_ref, state_ref,
    real_ref, last_ref, uses_ref, pair_ref,
    swap_out, swap_in, out1, in1, out3, in3, back_out, back_in,
    load_sems, store_sems, swap_sems, send1, recv1, send3, recv3, back_sems,
):
    blocks = tiles // PER
    half = heads * HEAD // 2
    chips = outer * inner // 2
    part = half // chips
    me = lax.axis_index("outer") * inner + lax.axis_index("inner")
    chip = me // 2
    core = me % 2
    wide = heads * HEAD // chunks
    per_chunk = heads // chunks

    def place(device):
        return (device // inner, device % inner)

    def ahead(k):
        return (chip + k) % chips

    def chunk_at(c):
        return ((1 - core) * (chunks // 2) + c) % chunks

    def load(array, c):
        source = (key_hbm, value_hbm, query_hbm)[array]
        target = (key_ref, value_ref, query_ref)[array]
        index = c if array == 2 else chunk_at(c)
        cols = pl.ds(pl.multiple_of(index * wide, wide), wide)
        return pltpu.make_async_copy(
            source.at[:, cols], target.at[:, cols], load_sems.at[array, c]
        )

    for c in range(chunks):
        load(0, c).start()
        load(1, c).start()
    for c in range(chunks):
        load(2, c).start()

    twin = place(chip * 2 + 1 - core)
    barrier = pltpu.get_barrier_semaphore()
    pl.semaphore_signal(barrier, inc=1, device_id=twin, device_id_type=MESH)

    def greet(k, _):
        pl.semaphore_signal(
            barrier, inc=1, device_id=place(ahead(k) * 2 + core), device_id_type=MESH
        )
        return 0

    lax.fori_loop(1, chips, greet, 0)

    build_masks(tiles, doc_ref, fill_ref, real_ref, last_ref, uses_ref, pair_ref)

    def joins(block):
        closing = doc_ref[block * PER + PER - 1]
        return (closing == doc_ref[block * PER - 1]).astype(F32)

    def columns(head):
        return pl.ds(pl.multiple_of(head * HEAD, HEAD), HEAD)

    def added(head, block):
        rows = pl.ds(block * BLOCK, BLOCK)
        cols = columns(head)
        masked = value_ref[rows, cols] * last_ref[rows, :]
        return dot(key_ref[rows, cols], masked, ((0,), (0,)))

    def summed(c):
        load(0, c).wait()
        load(1, c).wait()

        def step(i, _):
            head = chunk_at(c) * per_chunk + i
            total = added(head, 0)
            for block in range(1, blocks):
                total = added(head, block) + joins(block) * total
            state_ref[columns(head), :] = total
            return 0

        lax.fori_loop(0, per_chunk, step, 0)

    for c in range(chunks // 2):
        summed(c)
    my_doc = jnp.full((8, HEAD), doc_ref[tiles - 1], jnp.int32).astype(F32)
    swap_out[pl.ds(0, half), :] = state_ref[pl.ds((1 - core) * half, half), :]
    swap_out[pl.ds(half, 8), :] = my_doc
    pl.semaphore_wait(barrier, chips)
    swap = pltpu.make_async_remote_copy(
        swap_out, swap_in, swap_sems.at[0], swap_sems.at[1], device_id=twin, device_id_type=MESH
    )
    swap.start()
    for c in range(chunks // 2, chunks):
        summed(c)
    swap.wait()

    first_core = core == 0
    their_doc = swap_in[pl.ds(half, 8), :]
    doc0 = jnp.where(first_core, my_doc, their_doc)
    doc1 = jnp.where(first_core, their_doc, my_doc)
    keep1 = (doc0 == doc1).astype(F32)[0:1, :]

    def pack(j, _):
        mine = state_ref[pl.ds(core * half + j * part, part), :]
        theirs = swap_in[pl.ds(j * part, part), :]
        state0 = jnp.where(first_core, mine, theirs)
        state1 = jnp.where(first_core, theirs, mine)
        slot = (j - chip + chips) % chips
        out1[slot, pl.ds(0, part), :] = state1 + keep1 * state0
        out1[slot, pl.ds(part, 8), :] = doc1
        return 0

    lax.fori_loop(0, chips, pack, 0)

    def copy1(k):
        return pltpu.make_async_remote_copy(
            out1.at[k], in1.at[k], send1.at[k], recv1.at[k],
            device_id=place(ahead(k) * 2 + core), device_id_type=MESH,
        )

    def copy3(k):
        return pltpu.make_async_remote_copy(
            out3.at[k], in3.at[k], send3.at[k], recv3.at[k],
            device_id=place(ahead(k) * 2 + core), device_id_type=MESH,
        )

    def run(begin, end, action):
        def step(k, _):
            action(k)
            return 0

        lax.fori_loop(begin, end, step, 0)

    def store(head):
        cols = columns(head)
        return pltpu.make_async_copy(raw_ref.at[:, cols], raw_hbm.at[:, cols], store_sems.at[head])

    def local(head):
        cols = columns(head)
        carry = None
        for block in range(blocks):
            rows = pl.ds(block * BLOCK, BLOCK)
            query = query_ref[rows, cols] * real_ref[rows, :]
            key = key_ref[rows, cols]
            value = value_ref[rows, cols] * real_ref[rows, :]
            if block > 0:
                high, low = split(carry)
            for piece in range(BLOCK // HALF_BLOCK):
                begin = piece * HALF_BLOCK
                end = begin + HALF_BLOCK
                at = pl.ds(block * BLOCK + begin, HALF_BLOCK)
                scores = dot(query[begin:end], key[:end], ((1,), (1,)))
                keep = pair_ref[block, pl.ds(begin, HALF_BLOCK), pl.ds(0, end)]
                raw = dot(scores.astype(BF16) * keep, value[:end], ((1,), (0,)))
                if block > 0:
                    using = query[begin:end] * uses_ref[at, :]
                    raw = raw + (dot(using, high, ((1,), (0,))) + dot(using, low, ((1,), (0,))))
                raw_ref[at, cols] = raw
            if block < blocks - 1:
                fresh = added(head, block)
                carry = fresh if block == 0 else fresh + joins(block) * carry
        store(head).start()

    run(1, chips, lambda k: copy1(k).start())
    in1[0] = out1[0]
    for c in range(chunks):
        load(2, c).wait()
    run(0, heads // 2, local)
    run(1, chips, lambda k: copy1(k).wait())

    def lap(c, so_far):
        total, doc = so_far
        to = (c - chip + chips) % chips
        slot = (chip - c + chips) % chips
        out3[to, pl.ds(0, part), :] = total
        out3[to, pl.ds(part, 8), :] = doc
        new_doc = in1[slot, pl.ds(part, 8), :]
        keep = (new_doc == doc).astype(F32)[0:1, :]
        return (in1[slot, pl.ds(0, part), :] + keep * total, new_doc)

    lax.fori_loop(
        0, chips, lap, (jnp.zeros((part, HEAD), F32), jnp.full((8, HEAD), -1.0, F32))
    )

    run(1, chips, lambda k: copy3(k).start())
    in3[0] = out3[0]
    run(heads // 2, heads, local)
    run(1, chips, lambda k: copy3(k).wait())

    before = in3[0, pl.ds(part, 8), :]
    keep0 = (doc0 == before).astype(F32)[0:1, :]
    prev_ref[...] = jnp.where(first_core, before, doc0)

    def unpack(k, _):
        source = (chip - k + chips) % chips
        entering = in3[k, pl.ds(0, part), :]
        rows = pl.ds(source * part, part)
        own_rows = pl.ds(core * half + source * part, part)
        state0 = jnp.where(first_core, state_ref[own_rows, :], swap_in[rows, :])
        between = state0 + keep0 * entering
        carry_ref[own_rows, :] = jnp.where(first_core, entering, between)
        back_out[rows, :] = jnp.where(first_core, between, entering)
        return 0

    lax.fori_loop(0, chips, unpack, 0)
    back = pltpu.make_async_remote_copy(
        back_out, back_in, back_sems.at[0], back_sems.at[1], device_id=twin, device_id_type=MESH
    )
    back.start()
    run(0, heads, lambda head: store(head).wait())
    back.wait()
    carry_ref[pl.ds((1 - core) * half, half), :] = back_in[...]


def local_part(mesh, queries, keys, values, tile_doc, tile_fill):
    outer, inner = mesh.shape["outer"], mesh.shape["inner"]
    length, width = queries.shape
    heads = width // HEAD
    chunks = 4
    chips = outer * inner // 2
    half = width // 2
    part = half // chips
    vmem = pl.BlockSpec(memory_space=pltpu.VMEM)
    smem = pl.BlockSpec(memory_space=pltpu.SMEM)
    hbm = pl.BlockSpec(memory_space=pl.ANY)
    slots = pltpu.VMEM((chips, part + 8, HEAD), F32)
    halves = pltpu.VMEM((half, HEAD), F32)
    swaps = pltpu.VMEM((half + 8, HEAD), F32)
    rows = pltpu.VMEM((length, width), BF16)
    mask = pltpu.VMEM((length, HEAD), BF16)
    sems = pltpu.SemaphoreType.DMA((chips,))
    pair = pltpu.SemaphoreType.DMA((2,))
    return pl.pallas_call(
        functools.partial(local_kernel, outer, inner, length // TILE, heads, chunks),
        in_specs=[smem, smem, hbm, hbm, hbm],
        out_specs=[hbm, vmem, vmem],
        out_shape=[
            jax.ShapeDtypeStruct((length, width), F32),
            jax.ShapeDtypeStruct((width, HEAD), F32),
            jax.ShapeDtypeStruct((8, HEAD), F32),
        ],
        scratch_shapes=[
            rows, rows, rows,
            pltpu.VMEM((length, width), F32),
            pltpu.VMEM((width, HEAD), F32),
            mask, mask, mask,
            pltpu.VMEM((length // BLOCK, BLOCK, BLOCK), BF16),
            swaps, swaps, slots, slots, slots, slots, halves, halves,
            pltpu.SemaphoreType.DMA((3, chunks)),
            pltpu.SemaphoreType.DMA((heads,)),
            pair, sems, sems, sems, sems, pair,
        ],
        compiler_params=pltpu.CompilerParams(
            collective_id=0, has_side_effects=True, vmem_limit_bytes=56 * 1024 * 1024
        ),
        name="local_part",
    )(tile_doc, tile_fill, queries, keys, values)


def finish_kernel(
    tiles, per_step,
    doc_ref, fill_ref, prev_ref, query_ref, raw_ref, carry_ref, gain_ref, out_ref, uses_ref,
):
    @pl.when(pl.program_id(0) == 0)
    def _():
        entering = prev_ref[0:1, :]
        for tile in range(tiles):
            doc = jnp.full((1, HEAD), doc_ref[tile], jnp.int32).astype(F32)
            same = (doc == entering).astype(F32)
            real = rows_below(fill_ref[tile]).astype(F32)
            uses_ref[pl.ds(tile * TILE, TILE), :] = (real * same).astype(BF16)

    for head in range(per_step):
        cols = slice(head * HEAD, (head + 1) * HEAD)
        high, low = split(carry_ref[cols, :])
        using = query_ref[:, cols] * uses_ref[...]
        raw = raw_ref[:, cols]
        raw = raw + (dot(using, high, ((1,), (0,))) + dot(using, low, ((1,), (0,))))
        meansq = jnp.mean(raw * raw, axis=-1, keepdims=True)
        out_ref[:, cols] = (raw * lax.rsqrt(meansq + 1e-06) * gain_ref[:, cols]).astype(BF16)


def finish(queries, raw, gain, tile_doc, tile_fill, carry, prev):
    length, width = queries.shape
    heads = width // HEAD
    per_step = 2
    block = pl.BlockSpec((length, per_step * HEAD), lambda h: (0, h))
    smem = pl.BlockSpec(memory_space=pltpu.SMEM)
    return pl.pallas_call(
        functools.partial(finish_kernel, length // TILE, per_step),
        grid=(heads // per_step,),
        in_specs=[
            smem,
            smem,
            pl.BlockSpec((8, HEAD), lambda h: (0, 0)),
            block,
            block,
            pl.BlockSpec((per_step * HEAD, HEAD), lambda h: (h, 0)),
            pl.BlockSpec((1, per_step * HEAD), lambda h: (0, h)),
        ],
        out_specs=block,
        out_shape=jax.ShapeDtypeStruct((length, width), BF16),
        scratch_shapes=[pltpu.VMEM((length, HEAD), BF16)],
        compiler_params=pltpu.CompilerParams(vmem_limit_bytes=56 * 1024 * 1024),
        name="finish",
    )(tile_doc, tile_fill, prev, queries, raw, carry, gain.reshape(1, width))


def solution(mesh):
    def body(queries, keys, values, gain, tile_doc, tile_fill):
        raw, carry, prev = local_part(mesh, queries, keys, values, tile_doc, tile_fill)
        return finish(queries, raw, gain, tile_doc, tile_fill, carry, prev)

    rows = P(("outer", "inner"), None)
    tiles = P(("outer", "inner"))
    return jax.shard_map(
        body, mesh=mesh, in_specs=(rows, rows, rows, P(), tiles, tiles), out_specs=rows,
        check_vma=False,
    )
```

```python
import functools

import jax
import jax.numpy as jnp
from jax import lax
from jax.experimental import pallas as pl
from jax.experimental.pallas import tpu as pltpu
from jax.sharding import PartitionSpec as P

HEAD = 128
TILE = 128
BLOCK = 512
HALF_BLOCK = 256
PER = BLOCK // TILE
MESH = pl.DeviceIdType.MESH
F32 = jnp.float32
BF16 = jnp.bfloat16


def dot(a, b, dims):
    return lax.dot_general(a, b, (dims, ((), ())), preferred_element_type=F32)


def rows_below(limit):
    rows = lax.broadcasted_iota(jnp.int32, (TILE, HEAD), 0)
    return (rows < limit).astype(F32).astype(BF16)


def split(value):
    high = value.astype(BF16)
    return jnp.concatenate([high, (value - high.astype(F32)).astype(BF16)], axis=0)


def build_masks(tiles, doc_ref, fill_ref, real_ref, last_ref, uses_ref, pair_ref):
    for tile in range(tiles):
        block = tile // PER
        rows = pl.ds(tile * TILE, TILE)
        doc = doc_ref[tile]
        fill = fill_ref[tile]
        real_ref[rows, :] = rows_below(fill)
        closing = doc_ref[block * PER + PER - 1]
        last_ref[rows, :] = rows_below(jnp.where(doc == closing, fill, 0))
        if block > 0:
            opening = doc_ref[block * PER - 1]
            uses_ref[rows, :] = rows_below(jnp.where(doc == opening, fill, 0))
    above = lax.broadcasted_iota(jnp.int32, (TILE, TILE), 0)
    across = lax.broadcasted_iota(jnp.int32, (TILE, TILE), 1)
    lower = (above >= across).astype(F32).astype(BF16)
    for block in range(tiles // PER):
        for i in range(PER):
            for j in range(PER):
                spot = (block, pl.ds(i * TILE, TILE), pl.ds(j * TILE, TILE))
                if j > i:
                    pair_ref[spot] = jnp.zeros((TILE, TILE), BF16)
                elif j == i:
                    pair_ref[spot] = lower
                else:
                    same = doc_ref[block * PER + i] == doc_ref[block * PER + j]
                    pair_ref[spot] = rows_below(jnp.where(same, TILE, 0))


def local_kernel(
    outer, inner, tiles, heads, chunks,
    doc_ref, fill_ref, query_hbm, key_hbm, value_hbm, raw_ref, query_ref, carry_ref, prev_ref,
    key_ref, value_ref, state_ref,
    real_ref, last_ref, uses_ref, pair_ref,
    swap_out, swap_in, out1, in1, out3, in3, back_out, back_in,
    load_sems, swap_sems, send1, recv1, send3, recv3, back_sems,
):
    blocks = tiles // PER
    half = heads * HEAD // 2
    chips = outer * inner // 2
    part = half // chips
    me = lax.axis_index("outer") * inner + lax.axis_index("inner")
    chip = me // 2
    core = me % 2
    wide = heads * HEAD // chunks
    per_chunk = heads // chunks

    def place(device):
        return (device // inner, device % inner)

    def ahead(k):
        return (chip + k) % chips

    def chunk_at(c):
        return ((1 - core) * (chunks // 2) + c) % chunks

    def load(array, c):
        source = (key_hbm, value_hbm, query_hbm)[array]
        target = (key_ref, value_ref, query_ref)[array]
        index = c if array == 2 else chunk_at(c)
        cols = pl.ds(pl.multiple_of(index * wide, wide), wide)
        return pltpu.make_async_copy(
            source.at[:, cols], target.at[:, cols], load_sems.at[array, c]
        )

    for c in range(chunks):
        load(0, c).start()
        load(1, c).start()
    for c in range(chunks):
        load(2, c).start()

    twin = place(chip * 2 + 1 - core)
    barrier = pltpu.get_barrier_semaphore()
    pl.semaphore_signal(barrier, inc=1, device_id=twin, device_id_type=MESH)

    def greet(k, _):
        pl.semaphore_signal(
            barrier, inc=1, device_id=place(ahead(k) * 2 + core), device_id_type=MESH
        )
        return 0

    lax.fori_loop(1, chips, greet, 0)

    build_masks(tiles, doc_ref, fill_ref, real_ref, last_ref, uses_ref, pair_ref)

    def joins(block):
        closing = doc_ref[block * PER + PER - 1]
        return (closing == doc_ref[block * PER - 1]).astype(F32)

    def columns(head):
        return pl.ds(pl.multiple_of(head * HEAD, HEAD), HEAD)

    def added(head, block):
        rows = pl.ds(block * BLOCK, BLOCK)
        cols = columns(head)
        masked = value_ref[rows, cols] * last_ref[rows, :]
        return dot(key_ref[rows, cols], masked, ((0,), (0,)))

    def summed(c):
        load(0, c).wait()
        load(1, c).wait()

        def step(i, _):
            head = chunk_at(c) * per_chunk + i
            total = added(head, 0)
            for block in range(1, blocks):
                total = added(head, block) + joins(block) * total
            state_ref[columns(head), :] = total
            return 0

        lax.fori_loop(0, per_chunk, step, 0)

    for c in range(chunks // 2):
        summed(c)
    my_doc = jnp.full((8, HEAD), doc_ref[tiles - 1], jnp.int32).astype(F32)
    swap_out[pl.ds(0, half), :] = state_ref[pl.ds((1 - core) * half, half), :]
    swap_out[pl.ds(half, 8), :] = my_doc
    pl.semaphore_wait(barrier, chips)
    swap = pltpu.make_async_remote_copy(
        swap_out, swap_in, swap_sems.at[0], swap_sems.at[1], device_id=twin, device_id_type=MESH
    )
    swap.start()
    for c in range(chunks // 2, chunks):
        summed(c)
    swap.wait()

    first_core = core == 0
    their_doc = swap_in[pl.ds(half, 8), :]
    doc0 = jnp.where(first_core, my_doc, their_doc)
    doc1 = jnp.where(first_core, their_doc, my_doc)
    keep1 = (doc0 == doc1).astype(F32)[0:1, :]

    def pack(j, _):
        mine = state_ref[pl.ds(core * half + j * part, part), :]
        theirs = swap_in[pl.ds(j * part, part), :]
        state0 = jnp.where(first_core, mine, theirs)
        state1 = jnp.where(first_core, theirs, mine)
        slot = (j - chip + chips) % chips
        out1[slot, pl.ds(0, part), :] = state1 + keep1 * state0
        out1[slot, pl.ds(part, 8), :] = doc1
        return 0

    lax.fori_loop(0, chips, pack, 0)

    def copy1(k):
        return pltpu.make_async_remote_copy(
            out1.at[k], in1.at[k], send1.at[k], recv1.at[k],
            device_id=place(ahead(k) * 2 + core), device_id_type=MESH,
        )

    def copy3(k):
        return pltpu.make_async_remote_copy(
            out3.at[k], in3.at[k], send3.at[k], recv3.at[k],
            device_id=place(ahead(k) * 2 + core), device_id_type=MESH,
        )

    def run(begin, end, action):
        def step(k, _):
            action(k)
            return 0

        lax.fori_loop(begin, end, step, 0)

    def local(head):
        cols = columns(head)
        carry = None
        for block in range(blocks):
            rows = pl.ds(block * BLOCK, BLOCK)
            query = query_ref[rows, cols] * real_ref[rows, :]
            key = key_ref[rows, cols]
            value = value_ref[rows, cols] * real_ref[rows, :]
            if block > 0:
                parts = split(carry)
            for piece in range(BLOCK // HALF_BLOCK):
                begin = piece * HALF_BLOCK
                end = begin + HALF_BLOCK
                at = pl.ds(block * BLOCK + begin, HALF_BLOCK)
                scores = dot(query[begin:end], key[:end], ((1,), (1,)))
                keep = pair_ref[block, pl.ds(begin, HALF_BLOCK), pl.ds(0, end)]
                raw = dot(scores.astype(BF16) * keep, value[:end], ((1,), (0,)))
                if block > 0:
                    using = query[begin:end] * uses_ref[at, :]
                    twice = jnp.concatenate([using, using], axis=1)
                    raw = raw + dot(twice, parts, ((1,), (0,)))
                raw_ref[at, cols] = raw
            if block < blocks - 1:
                fresh = added(head, block)
                carry = fresh if block == 0 else fresh + joins(block) * carry

    run(1, chips, lambda k: copy1(k).start())
    in1[0] = out1[0]
    for c in range(chunks):
        load(2, c).wait()
    run(0, heads // 2, local)
    run(1, chips, lambda k: copy1(k).wait())

    def lap(c, so_far):
        total, doc = so_far
        to = (c - chip + chips) % chips
        slot = (chip - c + chips) % chips
        out3[to, pl.ds(0, part), :] = total
        out3[to, pl.ds(part, 8), :] = doc
        new_doc = in1[slot, pl.ds(part, 8), :]
        keep = (new_doc == doc).astype(F32)[0:1, :]
        return (in1[slot, pl.ds(0, part), :] + keep * total, new_doc)

    lax.fori_loop(
        0, chips, lap, (jnp.zeros((part, HEAD), F32), jnp.full((8, HEAD), -1.0, F32))
    )

    run(1, chips, lambda k: copy3(k).start())
    in3[0] = out3[0]
    run(heads // 2, heads, local)
    run(1, chips, lambda k: copy3(k).wait())

    before = in3[0, pl.ds(part, 8), :]
    keep0 = (doc0 == before).astype(F32)[0:1, :]
    prev_ref[...] = jnp.where(first_core, before, doc0)

    def unpack(k, _):
        source = (chip - k + chips) % chips
        entering = in3[k, pl.ds(0, part), :]
        rows = pl.ds(source * part, part)
        own_rows = pl.ds(core * half + source * part, part)
        state0 = jnp.where(first_core, state_ref[own_rows, :], swap_in[rows, :])
        between = state0 + keep0 * entering
        carry_ref[own_rows, :] = jnp.where(first_core, entering, between)
        back_out[rows, :] = jnp.where(first_core, between, entering)
        return 0

    lax.fori_loop(0, chips, unpack, 0)
    back = pltpu.make_async_remote_copy(
        back_out, back_in, back_sems.at[0], back_sems.at[1], device_id=twin, device_id_type=MESH
    )
    back.start()
    back.wait()
    carry_ref[pl.ds((1 - core) * half, half), :] = back_in[...]


def local_part(mesh, queries, keys, values, tile_doc, tile_fill):
    outer, inner = mesh.shape["outer"], mesh.shape["inner"]
    length, width = queries.shape
    heads = width // HEAD
    chunks = 4
    chips = outer * inner // 2
    half = width // 2
    part = half // chips
    vmem = pl.BlockSpec(memory_space=pltpu.VMEM)
    smem = pl.BlockSpec(memory_space=pltpu.SMEM)
    hbm = pl.BlockSpec(memory_space=pl.ANY)
    slots = pltpu.VMEM((chips, part + 8, HEAD), F32)
    halves = pltpu.VMEM((half, HEAD), F32)
    swaps = pltpu.VMEM((half + 8, HEAD), F32)
    rows = pltpu.VMEM((length, width), BF16)
    mask = pltpu.VMEM((length, HEAD), BF16)
    sems = pltpu.SemaphoreType.DMA((chips,))
    pair = pltpu.SemaphoreType.DMA((2,))
    return pl.pallas_call(
        functools.partial(local_kernel, outer, inner, length // TILE, heads, chunks),
        in_specs=[smem, smem, hbm, hbm, hbm],
        out_specs=[vmem, vmem, vmem, vmem],
        out_shape=[
            pltpu.VMEM((length, width), F32),
            pltpu.VMEM((length, width), BF16),
            jax.ShapeDtypeStruct((width, HEAD), F32),
            jax.ShapeDtypeStruct((8, HEAD), F32),
        ],
        scratch_shapes=[
            rows, rows,
            pltpu.VMEM((width, HEAD), F32),
            mask, mask, mask,
            pltpu.VMEM((length // BLOCK, BLOCK, BLOCK), BF16),
            swaps, swaps, slots, slots, slots, slots, halves, halves,
            pltpu.SemaphoreType.DMA((3, chunks)),
            pair, sems, sems, sems, sems, pair,
        ],
        compiler_params=pltpu.CompilerParams(
            collective_id=0, has_side_effects=True, vmem_limit_bytes=34 * 1024 * 1024
        ),
        name="local_part",
    )(tile_doc, tile_fill, queries, keys, values)


def finish_kernel(
    tiles, per_step,
    doc_ref, fill_ref, prev_ref, query_ref, raw_ref, carry_ref, gain_ref, out_ref, uses_ref,
):
    @pl.when(pl.program_id(0) == 0)
    def _():
        entering = prev_ref[0:1, :]
        for tile in range(tiles):
            doc = jnp.full((1, HEAD), doc_ref[tile], jnp.int32).astype(F32)
            same = (doc == entering).astype(F32)
            real = rows_below(fill_ref[tile]).astype(F32)
            uses_ref[pl.ds(tile * TILE, TILE), :] = (real * same).astype(BF16)

    for head in range(per_step):
        cols = slice(head * HEAD, (head + 1) * HEAD)
        begin = (pl.program_id(0) * per_step + head) * HEAD
        here = pl.ds(pl.multiple_of(begin, HEAD), HEAD)
        using = query_ref[:, here] * uses_ref[...]
        twice = jnp.concatenate([using, using], axis=1)
        raw = raw_ref[:, here]
        raw = raw + dot(twice, split(carry_ref[cols, :]), ((1,), (0,)))
        meansq = jnp.mean(raw * raw, axis=-1, keepdims=True)
        out_ref[:, cols] = (raw * lax.rsqrt(meansq + 1e-06) * gain_ref[:, cols]).astype(BF16)


def finish(queries, raw, gain, tile_doc, tile_fill, carry, prev):
    length, width = queries.shape
    heads = width // HEAD
    per_step = 2
    block = pl.BlockSpec((length, per_step * HEAD), lambda h: (0, h))
    smem = pl.BlockSpec(memory_space=pltpu.SMEM)
    return pl.pallas_call(
        functools.partial(finish_kernel, length // TILE, per_step),
        grid=(heads // per_step,),
        in_specs=[
            smem,
            smem,
            pl.BlockSpec((8, HEAD), lambda h: (0, 0)),
            pl.BlockSpec(memory_space=pltpu.VMEM),
            pl.BlockSpec(memory_space=pltpu.VMEM),
            pl.BlockSpec((per_step * HEAD, HEAD), lambda h: (h, 0)),
            pl.BlockSpec((1, per_step * HEAD), lambda h: (0, h)),
        ],
        out_specs=block,
        out_shape=jax.ShapeDtypeStruct((length, width), BF16),
        scratch_shapes=[pltpu.VMEM((length, HEAD), BF16)],
        compiler_params=pltpu.CompilerParams(vmem_limit_bytes=12 * 1024 * 1024),
        name="finish",
    )(tile_doc, tile_fill, prev, queries, raw, carry, gain.reshape(1, width))


def solution(mesh):
    def body(queries, keys, values, gain, tile_doc, tile_fill):
        raw, held, carry, prev = local_part(mesh, queries, keys, values, tile_doc, tile_fill)
        return finish(held, raw, gain, tile_doc, tile_fill, carry, prev)

    rows = P(("outer", "inner"), None)
    tiles = P(("outer", "inner"))
    return jax.shard_map(
        body, mesh=mesh, in_specs=(rows, rows, rows, P(), tiles, tiles), out_specs=rows,
        check_vma=False,
    )
```

```python
import functools

import jax
import jax.numpy as jnp
from jax import lax
from jax.experimental import pallas as pl
from jax.experimental.pallas import tpu as pltpu
from jax.sharding import PartitionSpec as P

HEAD = 128
TILE = 128
BLOCK = 512
HALF_BLOCK = 256
PER = BLOCK // TILE
MESH = pl.DeviceIdType.MESH
F32 = jnp.float32
BF16 = jnp.bfloat16


def dot(a, b, dims):
    return lax.dot_general(a, b, (dims, ((), ())), preferred_element_type=F32)


def rows_below(limit):
    rows = lax.broadcasted_iota(jnp.int32, (TILE, HEAD), 0)
    return (rows < limit).astype(F32).astype(BF16)


def split(value):
    high = value.astype(BF16)
    return jnp.concatenate([high, (value - high.astype(F32)).astype(BF16)], axis=0)


def build_masks(tiles, doc_ref, fill_ref, real_ref, last_ref, uses_ref, pair_ref):
    for tile in range(tiles):
        block = tile // PER
        rows = pl.ds(tile * TILE, TILE)
        doc = doc_ref[tile]
        fill = fill_ref[tile]
        real_ref[rows, :] = rows_below(fill)
        closing = doc_ref[block * PER + PER - 1]
        last_ref[rows, :] = rows_below(jnp.where(doc == closing, fill, 0))
        if block > 0:
            opening = doc_ref[block * PER - 1]
            uses_ref[rows, :] = rows_below(jnp.where(doc == opening, fill, 0))
    above = lax.broadcasted_iota(jnp.int32, (TILE, TILE), 0)
    across = lax.broadcasted_iota(jnp.int32, (TILE, TILE), 1)
    lower = (above >= across).astype(F32).astype(BF16)
    for block in range(tiles // PER):
        for i in range(PER):
            for j in range(PER):
                spot = (block, pl.ds(i * TILE, TILE), pl.ds(j * TILE, TILE))
                if j > i:
                    pair_ref[spot] = jnp.zeros((TILE, TILE), BF16)
                elif j == i:
                    pair_ref[spot] = lower
                else:
                    same = doc_ref[block * PER + i] == doc_ref[block * PER + j]
                    pair_ref[spot] = rows_below(jnp.where(same, TILE, 0))


def local_kernel(
    outer, inner, tiles, heads, chunks,
    doc_ref, fill_ref, query_hbm, key_hbm, value_hbm, raw_ref, query_ref, carry_ref, enters_ref,
    key_ref, value_ref, state_ref,
    real_ref, last_ref, uses_ref, pair_ref,
    swap_out, swap_in, out1, in1, out3, in3, back_out, back_in,
    load_sems, swap_sems, send1, recv1, send3, recv3, back_sems,
):
    blocks = tiles // PER
    half = heads * HEAD // 2
    chips = outer * inner // 2
    part = half // chips
    me = lax.axis_index("outer") * inner + lax.axis_index("inner")
    chip = me // 2
    core = me % 2
    wide = heads * HEAD // chunks
    per_chunk = heads // chunks

    def place(device):
        return (device // inner, device % inner)

    def ahead(k):
        return (chip + k) % chips

    def chunk_at(c):
        return ((1 - core) * (chunks // 2) + c) % chunks

    def load(array, c):
        source = (key_hbm, value_hbm, query_hbm)[array]
        target = (key_ref, value_ref, query_ref)[array]
        index = c if array == 2 else chunk_at(c)
        cols = pl.ds(pl.multiple_of(index * wide, wide), wide)
        return pltpu.make_async_copy(
            source.at[:, cols], target.at[:, cols], load_sems.at[array, c]
        )

    for c in range(chunks):
        load(0, c).start()
        load(1, c).start()
    for c in range(chunks):
        load(2, c).start()

    twin = place(chip * 2 + 1 - core)
    barrier = pltpu.get_barrier_semaphore()
    pl.semaphore_signal(barrier, inc=1, device_id=twin, device_id_type=MESH)

    def greet(k, _):
        pl.semaphore_signal(
            barrier, inc=1, device_id=place(ahead(k) * 2 + core), device_id_type=MESH
        )
        return 0

    lax.fori_loop(1, chips, greet, 0)

    build_masks(tiles, doc_ref, fill_ref, real_ref, last_ref, uses_ref, pair_ref)

    def joins(block):
        closing = doc_ref[block * PER + PER - 1]
        return (closing == doc_ref[block * PER - 1]).astype(F32)

    def columns(head):
        return pl.ds(pl.multiple_of(head * HEAD, HEAD), HEAD)

    def added(head, block):
        rows = pl.ds(block * BLOCK, BLOCK)
        cols = columns(head)
        masked = value_ref[rows, cols] * last_ref[rows, :]
        return dot(key_ref[rows, cols], masked, ((0,), (0,)))

    def summed(c):
        load(0, c).wait()
        load(1, c).wait()

        def step(i, _):
            head = chunk_at(c) * per_chunk + i
            total = added(head, 0)
            for block in range(1, blocks):
                total = added(head, block) + joins(block) * total
            state_ref[columns(head), :] = total
            return 0

        lax.fori_loop(0, per_chunk, step, 0)

    for c in range(chunks // 2):
        summed(c)
    my_doc = jnp.full((8, HEAD), doc_ref[tiles - 1], jnp.int32).astype(F32)
    swap_out[pl.ds(0, half), :] = state_ref[pl.ds((1 - core) * half, half), :]
    swap_out[pl.ds(half, 8), :] = my_doc
    pl.semaphore_wait(barrier, chips)
    swap = pltpu.make_async_remote_copy(
        swap_out, swap_in, swap_sems.at[0], swap_sems.at[1], device_id=twin, device_id_type=MESH
    )
    swap.start()
    for c in range(chunks // 2, chunks):
        summed(c)
    swap.wait()

    first_core = core == 0
    their_doc = swap_in[pl.ds(half, 8), :]
    doc0 = jnp.where(first_core, my_doc, their_doc)
    doc1 = jnp.where(first_core, their_doc, my_doc)
    keep1 = (doc0 == doc1).astype(F32)[0:1, :]

    def pack(j, _):
        mine = state_ref[pl.ds(core * half + j * part, part), :]
        theirs = swap_in[pl.ds(j * part, part), :]
        state0 = jnp.where(first_core, mine, theirs)
        state1 = jnp.where(first_core, theirs, mine)
        slot = (j - chip + chips) % chips
        out1[slot, pl.ds(0, part), :] = state1 + keep1 * state0
        out1[slot, pl.ds(part, 8), :] = doc1
        return 0

    lax.fori_loop(0, chips, pack, 0)

    def copy1(k):
        return pltpu.make_async_remote_copy(
            out1.at[k], in1.at[k], send1.at[k], recv1.at[k],
            device_id=place(ahead(k) * 2 + core), device_id_type=MESH,
        )

    def copy3(k):
        return pltpu.make_async_remote_copy(
            out3.at[k], in3.at[k], send3.at[k], recv3.at[k],
            device_id=place(ahead(k) * 2 + core), device_id_type=MESH,
        )

    def run(begin, end, action):
        def step(k, _):
            action(k)
            return 0

        lax.fori_loop(begin, end, step, 0)

    def local(head):
        cols = columns(head)
        carry = None
        for block in range(blocks):
            rows = pl.ds(block * BLOCK, BLOCK)
            query = query_ref[rows, cols] * real_ref[rows, :]
            key = key_ref[rows, cols]
            value = value_ref[rows, cols] * real_ref[rows, :]
            if block > 0:
                parts = split(carry)
            for piece in range(BLOCK // HALF_BLOCK):
                begin = piece * HALF_BLOCK
                end = begin + HALF_BLOCK
                at = pl.ds(block * BLOCK + begin, HALF_BLOCK)
                scores = dot(query[begin:end], key[:end], ((1,), (1,)))
                keep = pair_ref[block, pl.ds(begin, HALF_BLOCK), pl.ds(0, end)]
                raw = dot(scores.astype(BF16) * keep, value[:end], ((1,), (0,)))
                if block > 0:
                    using = query[begin:end] * uses_ref[at, :]
                    twice = jnp.concatenate([using, using], axis=1)
                    raw = raw + dot(twice, parts, ((1,), (0,)))
                raw_ref[at, cols] = raw
            if block < blocks - 1:
                fresh = added(head, block)
                carry = fresh if block == 0 else fresh + joins(block) * carry

    run(1, chips, lambda k: copy1(k).start())
    in1[0] = out1[0]
    for c in range(chunks):
        load(2, c).wait()
    early = (heads - 2) // 2
    run(0, early, local)
    run(1, chips, lambda k: copy1(k).wait())

    def lap(c, so_far):
        total, doc = so_far
        to = (c - chip + chips) % chips
        slot = (chip - c + chips) % chips
        out3[to, pl.ds(0, part), :] = total
        out3[to, pl.ds(part, 8), :] = doc
        new_doc = in1[slot, pl.ds(part, 8), :]
        keep = (new_doc == doc).astype(F32)[0:1, :]
        return (in1[slot, pl.ds(0, part), :] + keep * total, new_doc)

    lax.fori_loop(
        0, chips, lap, (jnp.zeros((part, HEAD), F32), jnp.full((8, HEAD), -1.0, F32))
    )

    run(1, chips, lambda k: copy3(k).start())
    in3[0] = out3[0]
    run(early, heads - 2, local)
    run(1, chips, lambda k: copy3(k).wait())

    before = in3[0, pl.ds(part, 8), :]
    keep0 = (doc0 == before).astype(F32)[0:1, :]
    entered = jnp.where(first_core, before, doc0)[0:1, :]

    def unpack(k, _):
        source = (chip - k + chips) % chips
        entering = in3[k, pl.ds(0, part), :]
        rows = pl.ds(source * part, part)
        own_rows = pl.ds(core * half + source * part, part)
        state0 = jnp.where(first_core, state_ref[own_rows, :], swap_in[rows, :])
        between = state0 + keep0 * entering
        carry_ref[own_rows, :] = jnp.where(first_core, entering, between)
        back_out[rows, :] = jnp.where(first_core, between, entering)
        return 0

    lax.fori_loop(0, chips, unpack, 0)
    back = pltpu.make_async_remote_copy(
        back_out, back_in, back_sems.at[0], back_sems.at[1], device_id=twin, device_id_type=MESH
    )
    back.start()
    for tile in range(tiles):
        rows = pl.ds(tile * TILE, TILE)
        doc = jnp.full((1, HEAD), doc_ref[tile], jnp.int32).astype(F32)
        same = (doc == entered).astype(F32)
        enters_ref[rows, :] = (real_ref[rows, :].astype(F32) * same).astype(BF16)
    run(heads - 2, heads, local)
    back.wait()
    carry_ref[pl.ds((1 - core) * half, half), :] = back_in[...]


def local_part(mesh, queries, keys, values, tile_doc, tile_fill):
    outer, inner = mesh.shape["outer"], mesh.shape["inner"]
    length, width = queries.shape
    heads = width // HEAD
    chunks = 4
    chips = outer * inner // 2
    half = width // 2
    part = half // chips
    vmem = pl.BlockSpec(memory_space=pltpu.VMEM)
    smem = pl.BlockSpec(memory_space=pltpu.SMEM)
    hbm = pl.BlockSpec(memory_space=pl.ANY)
    slots = pltpu.VMEM((chips, part + 8, HEAD), F32)
    halves = pltpu.VMEM((half, HEAD), F32)
    swaps = pltpu.VMEM((half + 8, HEAD), F32)
    rows = pltpu.VMEM((length, width), BF16)
    mask = pltpu.VMEM((length, HEAD), BF16)
    sems = pltpu.SemaphoreType.DMA((chips,))
    pair = pltpu.SemaphoreType.DMA((2,))
    return pl.pallas_call(
        functools.partial(local_kernel, outer, inner, length // TILE, heads, chunks),
        in_specs=[smem, smem, hbm, hbm, hbm],
        out_specs=[vmem, vmem, vmem, vmem],
        out_shape=[
            pltpu.VMEM((length, width), F32),
            pltpu.VMEM((length, width), BF16),
            jax.ShapeDtypeStruct((width, HEAD), F32),
            jax.ShapeDtypeStruct((length, HEAD), BF16),
        ],
        scratch_shapes=[
            rows, rows,
            pltpu.VMEM((width, HEAD), F32),
            mask, mask, mask,
            pltpu.VMEM((length // BLOCK, BLOCK, BLOCK), BF16),
            swaps, swaps, slots, slots, slots, slots, halves, halves,
            pltpu.SemaphoreType.DMA((3, chunks)),
            pair, sems, sems, sems, sems, pair,
        ],
        compiler_params=pltpu.CompilerParams(
            collective_id=0, has_side_effects=True, vmem_limit_bytes=34 * 1024 * 1024
        ),
        name="local_part",
    )(tile_doc, tile_fill, queries, keys, values)


def finish_kernel(per_step, enters_ref, query_ref, raw_ref, carry_ref, gain_ref, out_ref):
    for head in range(per_step):
        cols = slice(head * HEAD, (head + 1) * HEAD)
        begin = (pl.program_id(0) * per_step + head) * HEAD
        here = pl.ds(pl.multiple_of(begin, HEAD), HEAD)
        using = query_ref[:, here] * enters_ref[...]
        twice = jnp.concatenate([using, using], axis=1)
        raw = raw_ref[:, here]
        raw = raw + dot(twice, split(carry_ref[cols, :]), ((1,), (0,)))
        meansq = jnp.mean(raw * raw, axis=-1, keepdims=True)
        out_ref[:, cols] = (raw * lax.rsqrt(meansq + 1e-06) * gain_ref[:, cols]).astype(BF16)


def finish(queries, raw, gain, carry, enters):
    length, width = queries.shape
    heads = width // HEAD
    per_step = 2
    vmem = pl.BlockSpec(memory_space=pltpu.VMEM)
    return pl.pallas_call(
        functools.partial(finish_kernel, per_step),
        grid=(heads // per_step,),
        in_specs=[
            vmem,
            vmem,
            vmem,
            pl.BlockSpec((per_step * HEAD, HEAD), lambda h: (h, 0)),
            pl.BlockSpec((1, per_step * HEAD), lambda h: (0, h)),
        ],
        out_specs=pl.BlockSpec((length, per_step * HEAD), lambda h: (0, h)),
        out_shape=jax.ShapeDtypeStruct((length, width), BF16),
        compiler_params=pltpu.CompilerParams(vmem_limit_bytes=12 * 1024 * 1024),
        name="finish",
    )(enters, queries, raw, carry, gain.reshape(1, width))


def solution(mesh):
    def body(queries, keys, values, gain, tile_doc, tile_fill):
        raw, held, carry, enters = local_part(mesh, queries, keys, values, tile_doc, tile_fill)
        return finish(held, raw, gain, carry, enters)

    rows = P(("outer", "inner"), None)
    tiles = P(("outer", "inner"))
    return jax.shard_map(
        body, mesh=mesh, in_specs=(rows, rows, rows, P(), tiles, tiles), out_specs=rows,
        check_vma=False,
    )
```
